256 devices in a mesh: section: 8 (over z_lo, core), dp: 4 (over x), mp: 8 (over z_hi, y).
Axes of the slice: x: 4, y: 4, z: 8 (z_hi: 2, z_lo: 4; z = z_hi * 4 + z_lo), core: 2. Of those that a mesh axis runs over, the one named last changes fastest.
Arguments:
- taps: bfloat16 [4, 16, 64, 64, 4096], P(None, 'dp', 'mp', None, 'section'), may hold values from -6 to 6
- ln_gain: float32 [4, 4096], P(None, 'section'), may hold values from 0.1 to 1.9
- w_proj: bfloat16 [4, 4096, 256], P(None, ('section', 'dp', 'mp')), may hold values from -0.09375 to 0.09375
- conv_one: bfloat16 [2304, 256], P(('dp', 'mp')), may hold values from -0.125 to 0.125
- conv_two: bfloat16 [2304, 256], P(('dp', 'mp'), 'section'), may hold values from -0.125 to 0.125
Outputs:
- refined: bfloat16 [16, 64, 64, 256], P('dp', 'mp', None, 'section')
The draws below stay inside these ranges and needn't reach their ends.
All inputs are finite; a program needn't handle non-finite values.
Results may differ from the reference program's by a relative error of at most 0.023.
Values may be sent and summed in bfloat16 or wider, within the bound.
A program may use at most 128 MiB of HBM per device.

```python
import jax
import jax.numpy as jnp
from jax import lax

D = 4096
C = 256
GH = 64
GW = 64
TAPS = 4
IMGS = 16


def level_of(key, extent, pieces, smallest, largest):
    loudness, own = 1.0, jax.random.fold_in(key, 6)
    for dim, parts in pieces:
        draws = jnp.exp(jax.random.uniform(jax.random.fold_in(own, dim), (parts,), jnp.float32, smallest / len(pieces), largest / len(pieces)))
        loudness = loudness * jnp.repeat(draws, extent[dim] // parts).reshape([-1 if axis == dim else 1 for axis in range(len(extent))])
    return loudness


def gaussian(stream_key, extent, scale, bound, cuts=(), dtype=jnp.bfloat16):
    values = jax.random.normal(stream_key, extent, jnp.float32) * scale
    if len(cuts) > 0:
        values = level_of(stream_key, extent, cuts, -0.22, 0.18) * values
    return jnp.clip(values, min=-bound, max=bound).astype(dtype)


def setup_inputs(seed: int = 0) -> dict:
    streams_of = jax.random.split(jax.random.key(seed), 6)
    return {
        "taps": gaussian(streams_of[0], (TAPS, IMGS, GH, GW, D), 1.0, 6.0, ((1, 4), (2, 8), (4, 8))),
        "ln_gain": jnp.clip(1.0 + 0.18 * jax.random.normal(streams_of[1], (TAPS, D), jnp.float32), 0.1, 1.9),
        "w_proj": gaussian(streams_of[2], (TAPS, D, C), D ** -0.5, 0.09375, ((1, 256),)),
        "conv_one": gaussian(streams_of[3], (9 * C, C), (9 * C) ** -0.5, 0.125, ((0, 32),)),
        "conv_two": gaussian(streams_of[4], (9 * C, C), (9 * C) ** -0.5, 0.125, ((0, 32), (1, 8))),
    }


def convolve(act, weight):
    padded = jnp.pad(act, ((0, 0), (1, 1), (1, 1), (0, 0)))
    height = act.shape[1]
    width = act.shape[2]
    columns = jnp.concatenate([padded[:, a:a + height, b:b + width, :] for a in range(3) for b in range(3)], axis=-1)
    flat = columns.reshape(-1, columns.shape[-1])
    result = jnp.dot(flat, weight, preferred_element_type=jnp.float32)
    return result.reshape(act.shape[0], height, width, weight.shape[1])

def reference(taps, ln_gain, w_proj, conv_one, conv_two):
    joined = jnp.zeros((IMGS * GH * GW, C), jnp.float32)
    for layer in range(TAPS):
        values = taps[layer].astype(jnp.float32).reshape(-1, D)
        center = lax.optimization_barrier(jnp.mean(values, axis=-1, keepdims=True))
        spread = lax.optimization_barrier(jnp.mean(jnp.square(values - center), axis=-1, keepdims=True))
        normed = ((values - center) * jax.lax.rsqrt(spread + 1e-06) * ln_gain[layer]).astype(jnp.bfloat16)
        joined = joined + jnp.dot(normed, w_proj[layer], preferred_element_type=jnp.float32)
    joined = joined.reshape(IMGS, GH, GW, C)
    act_one = jnp.maximum(joined, 0.0).astype(jnp.bfloat16)
    act_two = jnp.maximum(convolve(act_one, conv_one), 0.0).astype(jnp.bfloat16)
    return (joined + convolve(act_two, conv_two)).astype(jnp.bfloat16)
```

```python
import jax
import jax.numpy as jnp
from jax import lax
from jax.experimental import pallas as pl
from jax.experimental.pallas import tpu as pltpu
from jax.sharding import PartitionSpec as P

D = 4096
TAPS = 4
MESH = pl.DeviceIdType.MESH
F32 = jnp.float32
BF16 = jnp.bfloat16


class Links:
    def __init__(self, send_sems, recv_sems):
        self.send_sems, self.recv_sems = send_sems, recv_sems
        self.used = 0
        self.copies = []

    def start(self, src, dst, to):
        copy = pltpu.make_async_remote_copy(
            src_ref=src,
            dst_ref=dst,
            send_sem=self.send_sems.at[self.used],
            recv_sem=self.recv_sems.at[self.used],
            device_id=to,
            device_id_type=MESH,
        )
        self.used += 1
        copy.start()
        self.copies.append(copy)
        return copy

    def finish(self):
        for copy in self.copies:
            copy.wait_send()


N_COPIES = 96


def kernel(
    taps_hbm, gain_ref, w_ref, c1_ref, c2_ref, out_ref,
    taps, part, wall, gw, gsum, gcol, c2pad, c2all, piece, call_, conv, tot, tparts, tred, tall, tcols,
    joint, jsib, jsum, jrecv, act, hsib, hcross, x1, x2, res, packed,
    tap_sems, send_sems, recv_sems,
):
    sec, x, mp = lax.axis_index("section"), lax.axis_index("dp"), lax.axis_index("mp")
    zlo, core = sec // 2, sec % 2
    zhi, y = mp // 4, mp % 4
    links = Links(send_sems, recv_sems)

    reads = [pltpu.make_async_copy(taps_hbm.at[t], taps.at[t], tap_sems.at[t]) for t in range(TAPS)]
    for read in reads:
        read.start()

    peers = [{"section": (sec + k) % 8} for k in range(1, 8)]
    x_up, x_down = {"dp": (x + 1) % 4}, {"dp": (x + 3) % 4}
    y_up, y_down = {"mp": zhi * 4 + (y + 1) % 4}, {"mp": zhi * 4 + (y + 3) % 4}
    z_far = {"mp": (1 - zhi) * 4 + y}
    cross = {"mp": (mp + 7 + 2 * core) % 8, "section": zlo * 2 + 1 - core}
    sibling = {"section": zlo * 2 + 1 - core}

    barrier = pltpu.get_barrier_semaphore()
    greeted = peers + [x_up, x_down, y_up, y_down, z_far, cross]
    for device in greeted:
        pl.semaphore_signal(barrier, inc=1, device_id=device, device_id_type=MESH)

    c2pad[...] = jnp.zeros_like(c2pad)
    c2pad[0:72, 0:32] = c2_ref[...]
    for t in range(TAPS):
        wall[t, x, zhi, y] = w_ref[t]
    pl.semaphore_wait(barrier, len(greeted))

    w_far = links.start(wall.at[:, x, zhi, y], wall.at[:, x, zhi, y], z_far)
    c2_got = [links.start(c2pad, c2all.at[k], peers[k - 1]) for k in range(1, 8)]

    lane = lax.broadcasted_iota(jnp.int32, (128, 128), 1)

    def stats(t, total):
        def body(b, total):
            v = taps[t, pl.ds(pl.multiple_of(b * 128, 128), 128), :].astype(F32)
            s = jnp.sum(v, axis=1, keepdims=True)
            q = jnp.sum(v * v, axis=1, keepdims=True)
            total = jnp.where(lane == b * 8 + t, s, total)
            return jnp.where(lane == b * 8 + 4 + t, q, total)

        return lax.fori_loop(0, 16, body, total)

    def w_first(part_, i, j):
        return wall.at[part_, i, :, j]

    class Spread:
        def __init__(self, view):
            self.view = view

        def begin(self):
            v = self.view
            a, b = v(0, None, x, y), v(1, None, x, y)
            self.a1, self.a2 = links.start(a, a, x_up), links.start(a, a, x_down)
            self.b1, self.b2 = links.start(b, b, y_up), links.start(b, b, y_down)

        def forward(self):
            v = self.view
            xm, xp, ym, yp = (x + 3) % 4, (x + 1) % 4, (y + 3) % 4, (y + 1) % 4
            self.a1.wait_recv()
            s = v(0, 0, xm, y)
            self.a3 = links.start(s, s, x_up)
            self.a2.wait_recv()
            s = v(0, 1, xp, y)
            self.a4 = links.start(s, s, x_down)
            self.b1.wait_recv()
            s = v(1, 0, x, ym)
            self.b3 = links.start(s, s, y_up)
            self.b2.wait_recv()
            s = v(1, 1, x, yp)
            self.b4 = links.start(s, s, y_down)

        def begin_second(self):
            v = self.view
            every = slice(None)
            self.a3.wait_recv()
            self.a4.wait_recv()
            a = v(0, None, every, y)
            self.a1, self.a2 = links.start(a, a, y_up), links.start(a, a, y_down)
            self.b3.wait_recv()
            self.b4.wait_recv()
            b = v(1, None, x, every)
            self.b1, self.b2 = links.start(b, b, x_up), links.start(b, b, x_down)

        def forward_second(self):
            v = self.view
            every = slice(None)
            xm, xp, ym, yp = (x + 3) % 4, (x + 1) % 4, (y + 3) % 4, (y + 1) % 4
            self.a1.wait_recv()
            s = v(0, 0, every, ym)
            self.a3 = links.start(s, s, y_up)
            self.a2.wait_recv()
            s = v(0, 1, every, yp)
            self.a4 = links.start(s, s, y_down)
            self.b1.wait_recv()
            s = v(1, 0, xm, every)
            self.b3 = links.start(s, s, x_up)
            self.b2.wait_recv()
            s = v(1, 1, xp, every)
            self.b4 = links.start(s, s, x_down)

        def finish(self):
            for copy in (self.a3, self.a4, self.b3, self.b4):
                copy.wait_recv()

    w_rows = {(0, None): slice(0, 2), (0, 0): slice(0, 1), (0, 1): slice(1, 2),
              (1, None): slice(2, 4), (1, 0): slice(2, 3), (1, 1): slice(3, 4)}
    c_rows = {(0, None): slice(0, 48), (0, 0): slice(0, 32), (0, 1): slice(32, 48),
              (1, None): slice(48, 80), (1, 0): slice(48, 64), (1, 1): slice(64, 80)}
    w_spread = Spread(lambda half, which, xs, ys: wall.at[w_rows[half, which], xs, :, ys])
    c_spread = Spread(lambda half, which, xs, ys: call_.at[core, xs, :, ys, c_rows[half, which]])

    reads[0].wait()
    total = stats(0, jnp.zeros((128, 128), F32))
    w_far.wait_recv()
    w_spread.begin()

    for copy in c2_got:
        copy.wait_recv()
    left, right = jnp.zeros((80, 128), F32), jnp.zeros((80, 128), F32)
    c2all[0] = c2pad[...]
    for d in range(8):
        block = c2all[(sec - d + 8) % 8].astype(F32)
        block = pltpu.roll(block, 32 * (d % 4), 1) if d % 4 else block
        if d < 4:
            left = left + block
        else:
            right = right + block
    first = jnp.concatenate([c1_ref[...].astype(F32), jnp.zeros((8, 256), F32)], axis=0)
    second = jnp.concatenate([left, right], axis=1)
    call_[core, x, zhi, y] = jnp.where(core == 0, first, second).astype(BF16)
    mine = call_.at[core, x, zhi, y]
    c_far = links.start(mine, mine, z_far)

    reads[1].wait()
    total = stats(1, total)
    w_spread.forward()
    reads[2].wait()
    total = stats(2, total)
    w_spread.begin_second()
    reads[3].wait()
    total = stats(3, total)
    tot[...] = total.T.reshape(8, 16, 128)
    sent = [links.start(tot.at[(sec + k) % 8], tparts.at[k], peers[k - 1]) for k in range(1, 8)]
    w_spread.forward_second()

    gcol[...] = jnp.zeros_like(gcol)
    gcol[0:4, :] = gain_ref[...]
    gains = gcol[...].T

    mine = tot[sec]
    for k in range(1, 8):
        sent[k - 1].wait_recv()
        mine = mine + tparts[k]
    outs = []
    for blk in range(2):
        mean = mine[8 * blk : 8 * blk + 4] / D
        var = jnp.maximum(mine[8 * blk + 4 : 8 * blk + 8] / D - mean * mean, 0.0)
        r = lax.rsqrt(var + 1e-6)
        outs += [r, r * mean]
    tall[sec] = jnp.concatenate(outs, axis=0)
    mine = tall.at[sec]
    sent = [links.start(mine, mine, peers[k - 1]) for k in range(1, 8)]

    c_far.wait_recv()
    c_spread.begin()
    w_spread.finish()

    for t in range(TAPS):
        scaled = (wall[t].reshape(512, 256).astype(F32) * gains[:, t : t + 1]).astype(BF16)
        gw[t] = scaled
        gsum[t] = jnp.sum(scaled.astype(F32), axis=0, keepdims=True)

        def project(i, _, t=t):
            rows = pl.ds(pl.multiple_of(i * 512, 512), 512)
            part[t, rows, :] = jnp.dot(taps[t, rows, :], gw[t], preferred_element_type=F32)
            return 0

        lax.fori_loop(0, 4, project, 0)
    c_spread.forward()

    for copy in sent:
        copy.wait_recv()
    tcols[...] = tall[...].reshape(128, 128).T

    def combine(b):
        cols = pltpu.roll(tcols[...], (128 - 8 * b) % 128, 1)
        rows = pl.ds(pl.multiple_of(b * 128, 128), 128)
        acc = cols[:, 0:1] * part[0, rows, :] - cols[:, 4:5] * gsum[0]
        for t in range(1, TAPS):
            acc = acc + (cols[:, t : t + 1] * part[t, rows, :] - cols[:, 4 + t : 5 + t] * gsum[t])
        return acc.astype(BF16)

    swaps = {}
    z_sent = {}

    def reduce(k):
        image = (zlo + k) % 4
        swaps[k].wait_recv()
        jsum[k] = (joint[image, core].astype(F32) + jsib[k].astype(F32)).astype(BF16)
        z_sent[k] = links.start(jsum.at[k], jrecv.at[k], {"section": (sec + 2 * k) % 8})

    for k in (1, 2, 3, 0):
        image = (zlo + k) % 4

        def strip(h, _, image=image):
            half = lax.rem(h + 1 - core + 2, 2)
            for blk in range(2):
                joint[image, half, blk * 128 : blk * 128 + 128] = combine(image * 4 + half * 2 + blk)
            return 0

        lax.fori_loop(0, 2, strip, 0)
        swaps[k] = links.start(joint.at[image, 1 - core], jsib.at[k], sibling)
        if k == 2:
            reduce(1)
        if k == 3:
            reduce(2)
        if k == 0:
            reduce(3)
    c_spread.begin_second()
    swaps[0].wait_recv()
    own = joint[zlo, core].astype(F32) + jsib[0].astype(F32)
    for k in range(1, 4):
        z_sent[k].wait_recv()
        own = own + jrecv[k].astype(F32)
    res[...] = own
    act[...] = jnp.maximum(own, 0.0).astype(BF16).reshape(2, 128, 256)
    h1 = links.start(act.at[1 - core], hsib, sibling)
    h2 = links.start(act.at[core], hcross, cross)
    c_spread.forward_second()
    c_spread.finish()
    whole = call_.at[core]
    c_swap = links.start(whole, whole, sibling)
    h1.wait_recv()
    h2.wait_recv()

    def columns(value, x_ref, rows):
        col = lax.broadcasted_iota(jnp.int32, (rows, 256), 0) % 64
        x_ref[:, 0:256] = jnp.where(col == 0, 0.0, pltpu.roll(value, 1, 0)).astype(BF16)
        x_ref[:, 256:512] = value.astype(BF16)
        x_ref[:, 512:768] = jnp.where(col == 63, 0.0, pltpu.roll(value, rows - 1, 0)).astype(BF16)

    top = jnp.logical_and(mp == 0, core == 0)
    bottom = jnp.logical_and(mp == 7, core == 1)
    near, far = hsib[...].astype(F32), hcross[...].astype(F32)
    above = jnp.where(core == 0, jnp.where(top, 0.0, far), near)
    below = jnp.where(core == 0, near, jnp.where(bottom, 0.0, far))
    columns(jnp.concatenate([above, jnp.maximum(res[...], 0.0), below], axis=0), x1, 512)

    c_swap.wait_recv()

    def unpack(which):
        def body(p, _):
            i, j, l = p // 4, (p // 2) % 2, 2 * (p % 2)
            one = call_[which, i, j, l].astype(F32)[0:72]
            two = call_[which, i, j, l + 1].astype(F32)[0:72]
            conv[which, pl.ds(pl.multiple_of(p * 144, 16), 144), :] = jnp.concatenate([one, two], axis=0).astype(BF16)
            return 0

        lax.fori_loop(0, 16, body, 0)

    unpack(0)
    mid = jnp.dot(x1[0:384], conv[0, 0:768], preferred_element_type=F32)
    mid = mid + jnp.dot(x1[64:448], conv[0, 768:1536], preferred_element_type=F32)
    mid = mid + jnp.dot(x1[128:512], conv[0, 1536:2304], preferred_element_type=F32)
    row = lax.broadcasted_iota(jnp.int32, (384, 256), 0)
    outside = jnp.logical_or(jnp.logical_and(top, row < 64), jnp.logical_and(bottom, row >= 320))
    columns(jnp.where(outside, 0.0, jnp.maximum(mid, 0.0)), x2, 384)
    unpack(1)
    fin = res[...] + jnp.dot(x2[0:256], conv[1, 0:768], preferred_element_type=F32)
    fin = fin + jnp.dot(x2[64:320], conv[1, 768:1536], preferred_element_type=F32)
    fin = fin + jnp.dot(x2[128:384], conv[1, 1536:2304], preferred_element_type=F32)

    group = lax.broadcasted_iota(jnp.int32, (64, 128), 1) // 32
    for d in range(8):
        got = jnp.zeros((64, 128), F32)
        for g in range(4):
            block = fin[64 * g : 64 * g + 64, 128 * (d // 4) : 128 * (d // 4) + 128]
            turn = (32 * (g - d % 4)) % 128
            block = pltpu.roll(block, turn, 1) if turn else block
            got = jnp.where(group == g, block, got)
        packed[d] = got.astype(BF16)
    outs = [links.start(packed.at[(sec + k) % 8], out_ref.at[sec], peers[k - 1]) for k in range(1, 8)]
    out_ref[sec] = packed[sec]
    for copy in outs:
        copy.wait_recv()
    links.finish()


def per_device(taps, ln_gain, w_proj, conv_one, conv_two):
    vmem = pl.BlockSpec(memory_space=pltpu.VMEM)
    out = pl.pallas_call(
        kernel,
        out_shape=jax.ShapeDtypeStruct((8, 64, 128), BF16),
        in_specs=[pl.BlockSpec(memory_space=pl.ANY)] + [vmem] * 4,
        out_specs=vmem,
        scratch_shapes=[
            pltpu.VMEM((4, 2048, 512), BF16),
            pltpu.VMEM((4, 2048, 256), F32),
            pltpu.VMEM((4, 4, 2, 4, 16, 256), BF16),
            pltpu.VMEM((4, 512, 256), BF16),
            pltpu.VMEM((4, 1, 256), F32),
            pltpu.VMEM((128, 512), F32),
            pltpu.VMEM((80, 128), BF16),
            pltpu.VMEM((8, 80, 128), BF16),
            pltpu.VMEM((80, 256), BF16),
            pltpu.VMEM((2, 4, 2, 4, 80, 256), BF16),
            pltpu.VMEM((2, 2304, 256), BF16),
            pltpu.VMEM((8, 16, 128), F32),
            pltpu.VMEM((8, 16, 128), F32),
            pltpu.VMEM((16, 128), F32),
            pltpu.VMEM((8, 16, 128), F32),
            pltpu.VMEM((128, 128), F32),
            pltpu.VMEM((4, 2, 256, 256), BF16),
            pltpu.VMEM((4, 256, 256), BF16),
            pltpu.VMEM((4, 256, 256), BF16),
            pltpu.VMEM((4, 256, 256), BF16),
            pltpu.VMEM((2, 128, 256), BF16),
            pltpu.VMEM((128, 256), BF16),
            pltpu.VMEM((128, 256), BF16),
            pltpu.VMEM((512, 768), BF16),
            pltpu.VMEM((384, 768), BF16),
            pltpu.VMEM((256, 256), F32),
            pltpu.VMEM((8, 64, 128), BF16),
            pltpu.SemaphoreType.DMA((TAPS,)),
            pltpu.SemaphoreType.DMA((N_COPIES,)),
            pltpu.SemaphoreType.DMA((N_COPIES,)),
        ],
        compiler_params=pltpu.CompilerParams(
            collective_id=0, has_side_effects=True, vmem_limit_bytes=56 * 1024 * 1024
        ),
        cost_estimate=pl.CostEstimate(flops=4_000_000_000, bytes_accessed=10_000_000, transcendentals=0),
    )(taps.reshape(4, 2048, 512), ln_gain, w_proj, conv_one, conv_two)
    return out.reshape(4, 2, 64, 4, 32).transpose(0, 1, 3, 2, 4).reshape(4, 8, 64, 32)


def solution(mesh):
    placed = (
        P(None, "dp", "mp", None, "section"),
        P(None, "section"),
        P(None, ("section", "dp", "mp"), None),
        P(("dp", "mp"), None),
        P(("dp", "mp"), "section"),
    )
    return jax.shard_map(
        per_device,
        mesh=mesh,
        in_specs=placed,
        out_specs=P("dp", "mp", None, "section"),
        check_vma=False,
    )
```

```python
import jax
import jax.numpy as jnp
from jax import lax
from jax.experimental import pallas as pl
from jax.experimental.pallas import tpu as pltpu
from jax.sharding import PartitionSpec as P

D = 4096
TAPS = 4
MESH = pl.DeviceIdType.MESH
F32 = jnp.float32
BF16 = jnp.bfloat16
N_COPIES = 80


class Links:
    def __init__(self, send_sems, recv_sems):
        self.send_sems, self.recv_sems = send_sems, recv_sems
        self.used = 0
        self.copies = []

    def make(self, src, dst, to, recv_sem=None):
        copy = pltpu.make_async_remote_copy(
            src_ref=src,
            dst_ref=dst,
            send_sem=self.send_sems.at[self.used],
            recv_sem=self.recv_sems.at[self.used] if recv_sem is None else recv_sem,
            device_id=to,
            device_id_type=MESH,
        )
        self.used += 1
        return copy

    def start(self, src, dst, to, recv_sem=None):
        copy = self.make(src, dst, to, recv_sem)
        copy.start()
        self.copies.append(copy)
        return copy

    def finish(self):
        for copy in self.copies:
            copy.wait_send()


def received(copies):
    for copy in copies:
        copy.wait_recv()


def kernel(
    taps_hbm, gain_ref, w_ref, c1_ref, c2_ref, out_ref,
    taps, part, wall, gw, gsum, gcol, c2sq, c2pad, c2all, call_, conv, tot, tparts, tall, tcols,
    joint, jsib, jsum, jrecv, act, hsib, hcross, x1, x2, res, packed, arrived,
    tap_sems, send_sems, recv_sems, line_sems,
):
    sec, x, mp = lax.axis_index("section"), lax.axis_index("dp"), lax.axis_index("mp")
    zlo, core = sec // 2, sec % 2
    zhi, y = mp // 4, mp % 4
    links = Links(send_sems, recv_sems)

    reads = [pltpu.make_async_copy(taps_hbm.at[t], taps.at[t], tap_sems.at[t]) for t in range(TAPS)]
    for read in reads:
        read.start()

    peers = [{"section": (sec + k) % 8} for k in range(1, 8)]
    xs = [{"dp": (x + k) % 4} for k in (1, 3, 2)]
    ys = [{"mp": zhi * 4 + (y + k) % 4} for k in (1, 3, 2)]
    z_far = {"mp": (1 - zhi) * 4 + y}
    sibling = {"section": zlo * 2 + 1 - core}
    has_cross = jnp.where(core == 0, mp > 0, mp < 7)
    cross = {"mp": (mp + 7 + 2 * core) % 8, "section": zlo * 2 + 1 - core}

    hcross[...] = jnp.zeros_like(hcross)
    jrecv[...] = jnp.zeros_like(jrecv)

    barrier = pltpu.get_barrier_semaphore()
    greeted = peers + xs + ys + [z_far]
    for device in greeted:
        pl.semaphore_signal(barrier, inc=1, device_id=device, device_id_type=MESH)

    @pl.when(has_cross)
    def _():
        pl.semaphore_signal(barrier, inc=1, device_id=cross, device_id_type=MESH)

    for t in range(TAPS):
        wall[t, x, zhi, y] = w_ref[t]
    c2sq[...] = jnp.zeros_like(c2sq)
    c2sq[0:32, 0:72] = c2_ref[...].astype(F32)
    rows = c2sq[...].T
    c2pad[...] = jnp.concatenate(
        [rows[0:24] + pltpu.roll(rows[24:48], 32, 1) + pltpu.roll(rows[48:72], 64, 1), jnp.zeros((8, 128), F32)], axis=0
    ).astype(BF16)
    gcol[...] = jnp.zeros_like(gcol)
    gcol[0:4, :] = gain_ref[...]
    pl.semaphore_wait(barrier, len(greeted) + has_cross.astype(jnp.int32))

    every = slice(None)

    def w_view(half, xi, yi, zi):
        return wall.at[2 * half : 2 * half + 2, xi, zi, yi]

    def c_view(half, xi, yi, zi):
        return call_.at[core, xi, zi, yi, (slice(0, 48), slice(48, 80))[half]]

    def first(view, zi):
        got = []
        for half, to in ((0, xs), (1, ys)):
            s = view(half, x, y, zi)
            got.append([links.start(s, s, device) for device in to])
        return got

    def second(view, zi, got):
        sent = []
        received(got[0])
        s = view(0, every, y, zi)
        sent += [links.start(s, s, device) for device in ys]
        received(got[1])
        s = view(1, x, every, zi)
        sent += [links.start(s, s, device) for device in xs]
        return sent

    mine = wall.at[:, x, zhi, y]
    w_far = links.start(mine, mine, z_far)
    w_near1 = first(w_view, zhi)

    lane = lax.broadcasted_iota(jnp.int32, (128, 128), 1)

    def stats(t, total):
        def body(b, total):
            v = taps[t, pl.ds(pl.multiple_of(b * 128, 128), 128), :].astype(F32)
            s = jnp.sum(v, axis=1, keepdims=True)
            q = jnp.sum(v * v, axis=1, keepdims=True)
            total = jnp.where(lane == b * 8 + t, s, total)
            return jnp.where(lane == b * 8 + 4 + t, q, total)

        return lax.fori_loop(0, 16, body, total)

    reads[0].wait()
    total = stats(0, jnp.zeros((128, 128), F32))
    reads[1].wait()
    total = stats(1, total)
    w_near2 = second(w_view, zhi, w_near1)
    w_far.wait_recv()
    w_far1 = first(w_view, 1 - zhi)
    reads[2].wait()
    total = stats(2, total)
    reads[3].wait()
    total = stats(3, total)
    tot[...] = total.T.reshape(8, 16, 128)
    sent = [links.start(tot.at[(sec + k) % 8], tparts.at[k], peers[k - 1]) for k in range(1, 8)]
    w_far2 = second(w_view, 1 - zhi, w_far1)
    c2_got = [links.start(c2pad, c2all.at[k], peers[k - 1]) for k in range(1, 8)]

    received(sent)
    own = tot[sec]
    for k in range(1, 8):
        own = own + tparts[k]
    outs = []
    for blk in range(2):
        mean = own[8 * blk : 8 * blk + 4] / D
        var = jnp.maximum(own[8 * blk + 4 : 8 * blk + 8] / D - mean * mean, 0.0)
        r = lax.rsqrt(var + 1e-6)
        outs += [r, r * mean]
    tall[sec] = jnp.concatenate(outs, axis=0)
    mine = tall.at[sec]
    sent = [links.start(mine, mine, peers[k - 1]) for k in range(1, 8)]

    received(c2_got)
    c2all[0] = c2pad[...]
    lanes24 = lax.broadcasted_iota(jnp.int32, (24, 128), 1) // 32
    sides = [[jnp.zeros((24, 128), F32) for _ in range(3)] for _ in range(2)]
    for d in range(8):
        block = c2all[(sec - d + 8) % 8].astype(F32)[0:24]
        for g in range(3):
            turn = (32 * (d % 4 - g)) % 128
            moved = pltpu.roll(block, turn, 1) if turn else block
            sides[d // 4][g] = jnp.where(lanes24 == d % 4, moved, sides[d // 4][g])
    blank = jnp.zeros((8, 256), F32)
    one = jnp.concatenate([c1_ref[...].astype(F32), blank], axis=0)
    two = jnp.concatenate([jnp.concatenate(side, axis=0) for side in sides], axis=1)
    two = jnp.concatenate([two, blank], axis=0)
    call_[core, x, zhi, y] = jnp.where(core == 0, one, two).astype(BF16)
    mine = call_.at[core, x, zhi, y]
    c_far = links.start(mine, mine, z_far)

    gains = gcol[...].T
    received(w_near2)
    received(w_far2)

    def project(t):
        scaled = (wall[t].reshape(512, 256).astype(F32) * gains[:, t : t + 1]).astype(BF16)
        gw[t] = scaled
        gsum[t] = jnp.sum(scaled.astype(F32), axis=0, keepdims=True)

        def body(i, _):
            rows = pl.ds(pl.multiple_of(i * 512, 512), 512)
            part[t, rows, :] = jnp.dot(taps[t, rows, :], gw[t], preferred_element_type=F32)
            return 0

        lax.fori_loop(0, 4, body, 0)

    project(0)
    project(1)
    c_far.wait_recv()
    c_got = first(c_view, every)
    project(2)
    project(3)

    received(sent)
    tcols[...] = tall[...].reshape(128, 128).T

    def combine(b):
        cols = pltpu.roll(tcols[...], (128 - 8 * b) % 128, 1)
        rows = pl.ds(pl.multiple_of(b * 128, 128), 128)
        acc = cols[:, 0:1] * part[0, rows, :] - cols[:, 4:5] * gsum[0]
        for t in range(1, TAPS):
            acc = acc + (cols[:, t : t + 1] * part[t, rows, :] - cols[:, 4 + t : 5 + t] * gsum[t])
        return acc.astype(BF16)

    def strips(image):
        def strip(h, _):
            half = lax.rem(h + 1 - core + 2, 2)
            for blk in range(2):
                joint[image, half, blk * 128 : blk * 128 + 128] = combine(image * 4 + half * 2 + blk)
            return 0

        lax.fori_loop(0, 2, strip, 0)

    place = jnp.where(zlo < 2, zlo, 3 - zlo)
    end = place == 0

    def absolute(p):
        return jnp.where(zlo < 2, p, 3 - p)

    images = [absolute(jnp.where(end, a, b)) for a, b in ((3, 2), (2, 0), (1, 3))] + [zlo]
    chips = [absolute(jnp.where(end, a, b)) for a, b in ((1, 2), (2, 0), (1, 3))]
    slots = [jnp.where(end, 4, zlo), zlo, zlo]

    def line_copy(k):
        return links.start(
            jsum.at[k], jrecv.at[slots[k]], {"section": chips[k] * 2 + core}, line_sems.at[slots[k]]
        )

    def line_arrived(slot):
        pltpu.make_async_remote_copy(
            src_ref=jsum.at[0], dst_ref=jrecv.at[slot], send_sem=send_sems.at[0], recv_sem=line_sems.at[slot],
            device_id=sibling, device_id_type=MESH,
        ).wait_recv()

    swaps = {}

    def onward(k):
        swaps[k].wait_recv()
        value = joint[images[k], core].astype(F32) + jsib[k].astype(F32)
        if k == 2:
            @pl.when(jnp.logical_not(end))
            def _():
                line_arrived(4)

            value = value + jrecv[4].astype(F32)
        jsum[k] = value.astype(BF16)
        line_copy(k)

    for k in range(4):
        strips(images[k])
        swaps[k] = links.start(joint.at[images[k], 1 - core], jsib.at[k], sibling)
        if k == 2:
            c_got = second(c_view, every, c_got)
        if k in (1, 2):
            onward(k - 1)
    onward(2)
    swaps[3].wait_recv()
    own = joint[zlo, core].astype(F32) + jsib[3].astype(F32)
    for s in range(4):
        far_end = 3 if s == 0 else 0 if s == 3 else -1

        @pl.when(jnp.logical_and(zlo != s, zlo != far_end))
        def _(s=s):
            line_arrived(s)

    for s in range(4):
        own = own + jrecv[s].astype(F32)
    res[...] = own
    act[...] = jnp.maximum(own, 0.0).astype(BF16).reshape(2, 128, 256)
    h1 = links.start(act.at[1 - core], hsib, sibling)
    h2 = links.make(act.at[core], hcross, cross)

    @pl.when(has_cross)
    def _():
        h2.start()

    received(c_got)
    whole = call_.at[core]
    c_swap = links.start(whole, whole, sibling)

    def unpack(which):
        def body(p, _):
            i, j, l = p // 4, (p // 2) % 2, 2 * (p % 2)
            one = call_[which, i, j, l].astype(F32)[0:72]
            two = call_[which, i, j, l + 1].astype(F32)[0:72]
            conv[which, pl.ds(pl.multiple_of(p * 144, 16), 144), :] = jnp.concatenate([one, two], axis=0).astype(BF16)
            return 0

        lax.fori_loop(0, 16, body, 0)

    unpack(core)
    c_swap.wait_recv()
    unpack(1 - core)
    h1.wait_recv()

    @pl.when(has_cross)
    def _():
        h2.wait_recv()
        h2.wait_send()

    def columns(value, x_ref, rows):
        col = lax.broadcasted_iota(jnp.int32, (rows, 256), 0) % 64
        x_ref[:, 0:256] = jnp.where(col == 0, 0.0, pltpu.roll(value, 1, 0)).astype(BF16)
        x_ref[:, 256:512] = value.astype(BF16)
        x_ref[:, 512:768] = jnp.where(col == 63, 0.0, pltpu.roll(value, rows - 1, 0)).astype(BF16)

    near, far = hsib[...].astype(F32), hcross[...].astype(F32)
    above = jnp.where(core == 0, far, near)
    below = jnp.where(core == 0, near, far)
    columns(jnp.concatenate([above, jnp.maximum(res[...], 0.0), below], axis=0), x1, 512)

    mid = jnp.dot(x1[0:384], conv[0, 0:768], preferred_element_type=F32)
    mid = mid + jnp.dot(x1[64:448], conv[0, 768:1536], preferred_element_type=F32)
    mid = mid + jnp.dot(x1[128:512], conv[0, 1536:2304], preferred_element_type=F32)
    row = lax.broadcasted_iota(jnp.int32, (384, 256), 0)
    top = jnp.logical_and(mp == 0, core == 0)
    bottom = jnp.logical_and(mp == 7, core == 1)
    outside = jnp.logical_or(jnp.logical_and(top, row < 64), jnp.logical_and(bottom, row >= 320))
    columns(jnp.where(outside, 0.0, jnp.maximum(mid, 0.0)), x2, 384)
    fin = res[...] + jnp.dot(x2[0:256], conv[1, 0:768], preferred_element_type=F32)
    fin = fin + jnp.dot(x2[64:320], conv[1, 768:1536], preferred_element_type=F32)
    fin = fin + jnp.dot(x2[128:384], conv[1, 1536:2304], preferred_element_type=F32)

    group = lax.broadcasted_iota(jnp.int32, (64, 128), 1) // 32
    for d in range(8):
        got = jnp.zeros((64, 128), F32)
        for g in range(4):
            block = fin[64 * g : 64 * g + 64, 128 * (d // 4) : 128 * (d // 4) + 128]
            turn = (32 * (g - d % 4)) % 128
            block = pltpu.roll(block, turn, 1) if turn else block
            got = jnp.where(group == g, block, got)
        packed[d] = got.astype(BF16)
    outs = [links.start(packed.at[(sec + k) % 8], arrived.at[k], peers[k - 1]) for k in range(1, 8)]
    arrived[0] = packed[sec]
    for k in range(8):
        if k:
            outs[k - 1].wait_recv()
        out_ref[(sec - k + 8) % 8] = arrived[k].astype(F32).T.astype(BF16)
    links.finish()


def per_device(taps, ln_gain, w_proj, conv_one, conv_two):
    vmem = pl.BlockSpec(memory_space=pltpu.VMEM)
    out = pl.pallas_call(
        kernel,
        out_shape=jax.ShapeDtypeStruct((8, 128, 64), BF16),
        in_specs=[pl.BlockSpec(memory_space=pl.ANY)] + [vmem] * 4,
        out_specs=vmem,
        scratch_shapes=[
            pltpu.VMEM((4, 2048, 512), BF16),
            pltpu.VMEM((4, 2048, 256), F32),
            pltpu.VMEM((4, 4, 2, 4, 16, 256), BF16),
            pltpu.VMEM((4, 512, 256), BF16),
            pltpu.VMEM((4, 1, 256), F32),
            pltpu.VMEM((128, 512), F32),
            pltpu.VMEM((128, 128), F32),
            pltpu.VMEM((32, 128), BF16),
            pltpu.VMEM((8, 32, 128), BF16),
            pltpu.VMEM((2, 4, 2, 4, 80, 256), BF16),
            pltpu.VMEM((2, 2304, 256), BF16),
            pltpu.VMEM((8, 16, 128), F32),
            pltpu.VMEM((8, 16, 128), F32),
            pltpu.VMEM((8, 16, 128), F32),
            pltpu.VMEM((128, 128), F32),
            pltpu.VMEM((4, 2, 256, 256), BF16),
            pltpu.VMEM((4, 256, 256), BF16),
            pltpu.VMEM((3, 256, 256), BF16),
            pltpu.VMEM((5, 256, 256), BF16),
            pltpu.VMEM((2, 128, 256), BF16),
            pltpu.VMEM((128, 256), BF16),
            pltpu.VMEM((128, 256), BF16),
            pltpu.VMEM((512, 768), BF16),
            pltpu.VMEM((384, 768), BF16),
            pltpu.VMEM((256, 256), F32),
            pltpu.VMEM((8, 64, 128), BF16),
            pltpu.VMEM((8, 64, 128), BF16),
            pltpu.SemaphoreType.DMA((TAPS,)),
            pltpu.SemaphoreType.DMA((N_COPIES,)),
            pltpu.SemaphoreType.DMA((N_COPIES,)),
            pltpu.SemaphoreType.DMA((5,)),
        ],
        compiler_params=pltpu.CompilerParams(
            collective_id=0, has_side_effects=True, vmem_limit_bytes=56 * 1024 * 1024
        ),
        cost_estimate=pl.CostEstimate(flops=4_000_000_000, bytes_accessed=10_000_000, transcendentals=0),
    )(taps.reshape(4, 2048, 512), ln_gain, w_proj, conv_one, conv_two.T)
    return out.reshape(4, 8, 32, 64).transpose(0, 1, 3, 2)


def solution(mesh):
    placed = (
        P(None, "dp", "mp", None, "section"),
        P(None, "section"),
        P(None, ("section", "dp", "mp"), None),
        P(("dp", "mp"), None),
        P(("dp", "mp"), "section"),
    )
    return jax.shard_map(
        per_device,
        mesh=mesh,
        in_specs=placed,
        out_specs=P("dp", "mp", None, "section"),
        check_vma=False,
    )
```

```python
import jax
import jax.numpy as jnp
from jax import lax
from jax.experimental import pallas as pl
from jax.experimental.pallas import tpu as pltpu
from jax.sharding import PartitionSpec as P

D = 4096
TAPS = 4
MESH = pl.DeviceIdType.MESH
F32 = jnp.float32
BF16 = jnp.bfloat16
N_COPIES = 112


class Links:
    def __init__(self, send_sems, recv_sems):
        self.send_sems, self.recv_sems = send_sems, recv_sems
        self.used = 0
        self.copies = []

    def make(self, src, dst, to, recv_sem=None):
        copy = pltpu.make_async_remote_copy(
            src_ref=src,
            dst_ref=dst,
            send_sem=self.send_sems.at[self.used],
            recv_sem=self.recv_sems.at[self.used] if recv_sem is None else recv_sem,
            device_id=to,
            device_id_type=MESH,
        )
        self.used += 1
        return copy

    def start(self, src, dst, to, recv_sem=None):
        copy = self.make(src, dst, to, recv_sem)
        copy.start()
        self.copies.append(copy)
        return copy

    def finish(self):
        for copy in self.copies:
            copy.wait_send()


def received(copies):
    for copy in copies:
        copy.wait_recv()


def kernel(
    taps_hbm, gain_ref, w_ref, c1_ref, c2_ref, out_ref,
    taps, part, wall, gw, gsum, gcol, c2sq, c2pad, c2all, call_, conv, tot, tparts, tall, tcols,
    joint, jsib, jsum, jrecv, act, hsib, hcross, x1, x2, res, packed, arrived,
    tap_sems, send_sems, recv_sems, line_sems,
):
    sec, x, mp = lax.axis_index("section"), lax.axis_index("dp"), lax.axis_index("mp")
    zlo, core = sec // 2, sec % 2
    zhi, y = mp // 4, mp % 4
    links = Links(send_sems, recv_sems)

    reads = [pltpu.make_async_copy(taps_hbm.at[t], taps.at[t], tap_sems.at[t]) for t in range(TAPS)]
    for read in reads:
        read.start()

    peers = [{"section": (sec + k) % 8} for k in range(1, 8)]
    xs = [{"dp": (x + k) % 4} for k in (1, 3, 2)]
    ys = [{"mp": zhi * 4 + (y + k) % 4} for k in (1, 3, 2)]
    plane = [
        {"dp": (x + i) % 4, "mp": zhi * 4 + (y + j) % 4} for i in range(4) for j in range(4) if i or j
    ]
    z_far = {"mp": (1 - zhi) * 4 + y}
    sibling = {"section": zlo * 2 + 1 - core}
    has_cross = jnp.where(core == 0, mp > 0, mp < 7)
    cross = {"mp": (mp + 7 + 2 * core) % 8, "section": zlo * 2 + 1 - core}

    hcross[...] = jnp.zeros_like(hcross)
    jrecv[...] = jnp.zeros_like(jrecv)

    barrier = pltpu.get_barrier_semaphore()
    greeted = peers + plane + [z_far]
    for device in greeted:
        pl.semaphore_signal(barrier, inc=1, device_id=device, device_id_type=MESH)

    @pl.when(has_cross)
    def _():
        pl.semaphore_signal(barrier, inc=1, device_id=cross, device_id_type=MESH)

    for t in range(TAPS):
        wall[t, x, zhi, y] = w_ref[t]
    pl.semaphore_wait(barrier, len(greeted) + has_cross.astype(jnp.int32))

    every = slice(None)

    def c_view(half, xi, yi, zi):
        return call_.at[core, xi, zi, yi, (slice(0, 48), slice(48, 80))[half]]

    def first(view, zi):
        got = []
        for half, to in ((0, xs), (1, ys)):
            s = view(half, x, y, zi)
            got.append([links.start(s, s, device) for device in to])
        return got

    def second(view, zi, got):
        sent = []
        received(got[0])
        s = view(0, every, y, zi)
        sent += [links.start(s, s, device) for device in ys]
        received(got[1])
        s = view(1, x, every, zi)
        sent += [links.start(s, s, device) for device in xs]
        return sent

    mine = wall.at[:, x, zhi, y]
    w_far = links.start(mine, mine, z_far)
    w_got = [links.start(mine, mine, device) for device in plane]

    lane = lax.broadcasted_iota(jnp.int32, (128, 128), 1)

    def stats(t, total):
        reads[t].wait()
        v = taps[t].astype(F32)
        s = jnp.sum(v, axis=1, keepdims=True)
        q = jnp.sum(v * v, axis=1, keepdims=True)
        for b in range(16):
            total = jnp.where(lane == b * 8 + t, s[128 * b : 128 * b + 128], total)
            total = jnp.where(lane == b * 8 + 4 + t, q[128 * b : 128 * b + 128], total)
        return total

    c2sq[...] = jnp.zeros_like(c2sq)
    c2sq[0:32, 0:72] = c2_ref[...].astype(F32)
    rows = c2sq[...].T
    c2pad[...] = jnp.concatenate(
        [rows[0:24] + pltpu.roll(rows[24:48], 32, 1) + pltpu.roll(rows[48:72], 64, 1), jnp.zeros((8, 128), F32)], axis=0
    ).astype(BF16)
    gcol[...] = jnp.zeros_like(gcol)
    gcol[0:4, :] = gain_ref[...]
    c2_got = [links.start(c2pad, c2all.at[k], peers[k - 1]) for k in range(1, 8)]

    total = jnp.zeros((128, 128), F32)
    for t in range(TAPS):
        total = stats(t, total)
    tot[...] = total.T.reshape(8, 16, 128)
    sent = [links.start(tot.at[(sec + k) % 8], tparts.at[k], peers[k - 1]) for k in range(1, 8)]
    w_far.wait_recv()
    mine = wall.at[:, x, 1 - zhi, y]
    w_got += [links.start(mine, mine, device) for device in plane]

    received(c2_got)
    c2all[0] = c2pad[...]
    lanes24 = lax.broadcasted_iota(jnp.int32, (24, 128), 1) // 32
    sides = [[jnp.zeros((24, 128), F32) for _ in range(3)] for _ in range(2)]
    for d in range(8):
        block = c2all[(sec - d + 8) % 8].astype(F32)[0:24]
        for g in range(3):
            turn = (32 * (d % 4 - g)) % 128
            moved = pltpu.roll(block, turn, 1) if turn else block
            sides[d // 4][g] = jnp.where(lanes24 == d % 4, moved, sides[d // 4][g])
    blank = jnp.zeros((8, 256), F32)
    one = jnp.concatenate([c1_ref[...].astype(F32), blank], axis=0)
    two = jnp.concatenate([jnp.concatenate(side, axis=0) for side in sides], axis=1)
    two = jnp.concatenate([two, blank], axis=0)
    call_[core, x, zhi, y] = jnp.where(core == 0, one, two).astype(BF16)
    mine = call_.at[core, x, zhi, y]
    c_far = links.start(mine, mine, z_far)

    received(sent)
    own = tot[sec]
    for k in range(1, 8):
        own = own + tparts[k]
    outs = []
    for blk in range(2):
        mean = own[8 * blk : 8 * blk + 4] / D
        var = jnp.maximum(own[8 * blk + 4 : 8 * blk + 8] / D - mean * mean, 0.0)
        r = lax.rsqrt(var + 1e-6)
        outs += [r, r * mean]
    tall[sec] = jnp.concatenate(outs, axis=0)
    mine = tall.at[sec]
    sent = [links.start(mine, mine, peers[k - 1]) for k in range(1, 8)]

    gains = gcol[...].T
    c_far.wait_recv()
    c_got = first(c_view, every)
    received(w_got)

    for t in range(TAPS):
        scaled = (wall[t].reshape(512, 256).astype(F32) * gains[:, t : t + 1]).astype(BF16)
        gw[t] = scaled
        gsum[t] = jnp.sum(scaled.astype(F32), axis=0, keepdims=True)

    received(sent)
    tcols[...] = tall[...].reshape(128, 128).T

    def strip(image, half):
        rows = pl.ds(pl.multiple_of(image * 512 + half * 256, 256), 256)
        for t in range(TAPS):
            part[t] = jnp.dot(taps[t, rows, :], gw[t], preferred_element_type=F32)
        for blk in range(2):
            cols = pltpu.roll(tcols[...], (128 - 8 * (image * 4 + half * 2 + blk)) % 128, 1)
            span = slice(blk * 128, blk * 128 + 128)
            acc = cols[:, 0:1] * part[0, span, :] - cols[:, 4:5] * gsum[0]
            for t in range(1, TAPS):
                acc = acc + (cols[:, t : t + 1] * part[t, span, :] - cols[:, 4 + t : 5 + t] * gsum[t])
            joint[image, half, span] = acc.astype(BF16)

    place = jnp.where(zlo < 2, zlo, 3 - zlo)
    end = place == 0

    def absolute(p):
        return jnp.where(zlo < 2, p, 3 - p)

    images = [absolute(jnp.where(end, a, b)) for a, b in ((3, 2), (2, 0), (1, 3))] + [zlo]
    chips = [absolute(jnp.where(end, a, b)) for a, b in ((1, 2), (2, 0), (1, 3))]
    slots = [jnp.where(end, 4, zlo), zlo, zlo]

    def line_send(k, h):
        links.start(
            jsum.at[k, h], jrecv.at[slots[k], h], {"section": chips[k] * 2 + core}, line_sems.at[slots[k], h]
        )

    def line_arrived(slot, h):
        pltpu.make_async_remote_copy(
            src_ref=jsum.at[0, 0], dst_ref=jrecv.at[slot, h], send_sem=send_sems.at[0],
            recv_sem=line_sems.at[slot, h], device_id=sibling, device_id_type=MESH,
        ).wait_recv()

    swaps = {}

    def swap(k):
        strip(images[k], 1 - core)
        swaps[k] = links.start(joint.at[images[k], 1 - core], jsib.at[k], sibling)

    def pair(k, h):
        span = pl.ds(pl.multiple_of(128 * h, 128), 128)
        return joint[images[k], core, span].astype(F32) + jsib[k, span].astype(F32)

    def onward(k):
        swaps[k].wait_recv()
        for h in halves:
            value = pair(k, h)
            if k == 2:
                @pl.when(jnp.logical_not(end))
                def _(h=h):
                    line_arrived(4, h)

                value = value + jrecv[4, h].astype(F32)
            jsum[k, h] = value.astype(BF16)
            line_send(k, h)

    def joined(h):
        for s in range(4):
            far_end = 3 if s == 0 else 0 if s == 3 else -1

            @pl.when(jnp.logical_and(zlo != s, zlo != far_end))
            def _(s=s):
                line_arrived(s, h)

        value = pair(3, h)
        for s in range(4):
            value = value + jrecv[s, h].astype(F32)
        res[h] = value
        act[h] = jnp.maximum(value, 0.0).astype(BF16)

    def unpack(which):
        def body(i, _):
            for j in range(2):
                for l in (0, 2):
                    one = call_[which, i, j, l].astype(F32)[0:72]
                    two = call_[which, i, j, l + 1].astype(F32)[0:72]
                    at = pl.ds(pl.multiple_of(i * 576, 16) + 288 * j + 72 * l, 144)
                    conv[which, at, :] = jnp.concatenate([one, two], axis=0).astype(BF16)
            return 0

        lax.fori_loop(0, 4, body, 0)

    halves = (core, 1 - core)
    swap(0)
    swap(1)
    strip(images[0], core)
    onward(0)
    c_got = second(c_view, every, c_got)
    swap(2)
    strip(images[1], core)
    onward(1)
    swap(3)
    strip(images[2], core)
    strip(images[3], core)
    onward(2)
    received(c_got)
    whole = call_.at[core]
    c_swap = links.start(whole, whole, sibling)
    swaps[3].wait_recv()
    joined(core)
    h2 = links.make(act.at[core], hcross, cross)

    @pl.when(has_cross)
    def _():
        h2.start()

    unpack(core)
    joined(1 - core)
    h1 = links.start(act.at[1 - core], hsib, sibling)
    c_swap.wait_recv()
    unpack(1 - core)

    def columns(value, x_ref, start):
        rows = value.shape[0]
        span = pl.ds(pl.multiple_of(start, 64), rows)
        col = lax.broadcasted_iota(jnp.int32, (rows, 256), 0) % 64
        x_ref[span, 0:256] = jnp.where(col == 0, 0.0, pltpu.roll(value, 1, 0)).astype(BF16)
        x_ref[span, 256:512] = value.astype(BF16)
        x_ref[span, 512:768] = jnp.where(col == 63, 0.0, pltpu.roll(value, rows - 1, 0)).astype(BF16)

    def convolved(x_ref, which, start, rows):
        total = jnp.zeros((rows, 256), F32)
        for a in range(3):
            span = pl.ds(pl.multiple_of(start + 64 * a, 64), rows)
            total = total + jnp.dot(
                x_ref[span], conv[which, 768 * a : 768 * a + 768], preferred_element_type=F32
            )
        return total

    def finished(which_half, p):
        total = convolved(x2, 1, 128 * which_half, 128) + res[which_half]
        packed[p] = total.T.astype(BF16).reshape(8, 32, 128)
        return [links.start(packed.at[p, (sec + k) % 8], arrived.at[p, k], peers[k - 1]) for k in range(1, 8)]

    columns(jnp.maximum(res[...].reshape(256, 256), 0.0), x1, 128)
    h1.wait_recv()
    columns(hsib[...].astype(F32), x1, 384 * (1 - core))
    columns(jnp.maximum(convolved(x1, 0, 128 * (1 - core), 256), 0.0), x2, 128 * (1 - core))
    outs = [finished(1 - core, 0)]

    @pl.when(has_cross)
    def _():
        h2.wait_recv()
        h2.wait_send()

    columns(hcross[...].astype(F32), x1, 384 * core)
    row = lax.broadcasted_iota(jnp.int32, (128, 256), 0) // 64
    outside = jnp.logical_and(row == core, jnp.logical_not(has_cross))
    mid = jnp.where(outside, 0.0, jnp.maximum(convolved(x1, 0, 256 * core, 128), 0.0))
    columns(mid, x2, 256 * core)
    outs.append(finished(core, 1))

    for p in range(2):
        arrived[p, 0] = packed[p, sec]
        for k in range(8):
            if k:
                outs[p][k - 1].wait_recv()
            their = (core + k) % 2
            block = arrived[p, k].astype(F32)
            for r, rows in ((0, block), (1, pltpu.roll(block, 64, 1))):
                at = 64 * (1 - their if p == 0 else their) + 32 * r
                out_ref[(sec - k + 8) % 8, pl.ds(pl.multiple_of(at, 32), 32), :] = rows[:, 0:64].astype(BF16)
    links.finish()


def per_device(taps, ln_gain, w_proj, conv_one, conv_two):
    vmem = pl.BlockSpec(memory_space=pltpu.VMEM)
    out = pl.pallas_call(
        kernel,
        out_shape=jax.ShapeDtypeStruct((8, 128, 64), BF16),
        in_specs=[pl.BlockSpec(memory_space=pl.ANY)] + [vmem] * 4,
        out_specs=vmem,
        scratch_shapes=[
            pltpu.VMEM((4, 2048, 512), BF16),
            pltpu.VMEM((4, 256, 256), F32),
            pltpu.VMEM((4, 4, 2, 4, 16, 256), BF16),
            pltpu.VMEM((4, 512, 256), BF16),
            pltpu.VMEM((4, 1, 256), F32),
            pltpu.VMEM((128, 512), F32),
            pltpu.VMEM((128, 128), F32),
            pltpu.VMEM((32, 128), BF16),
            pltpu.VMEM((8, 32, 128), BF16),
            pltpu.VMEM((2, 4, 2, 4, 80, 256), BF16),
            pltpu.VMEM((2, 2304, 256), BF16),
            pltpu.VMEM((8, 16, 128), F32),
            pltpu.VMEM((8, 16, 128), F32),
            pltpu.VMEM((8, 16, 128), F32),
            pltpu.VMEM((128, 128), F32),
            pltpu.VMEM((4, 2, 256, 256), BF16),
            pltpu.VMEM((4, 256, 256), BF16),
            pltpu.VMEM((3, 2, 128, 256), BF16),
            pltpu.VMEM((5, 2, 128, 256), BF16),
            pltpu.VMEM((2, 128, 256), BF16),
            pltpu.VMEM((128, 256), BF16),
            pltpu.VMEM((128, 256), BF16),
            pltpu.VMEM((512, 768), BF16),
            pltpu.VMEM((384, 768), BF16),
            pltpu.VMEM((2, 128, 256), F32),
            pltpu.VMEM((2, 8, 32, 128), BF16),
            pltpu.VMEM((2, 8, 32, 128), BF16),
            pltpu.SemaphoreType.DMA((TAPS,)),
            pltpu.SemaphoreType.DMA((N_COPIES,)),
            pltpu.SemaphoreType.DMA((N_COPIES,)),
            pltpu.SemaphoreType.DMA((5, 2)),
        ],
        compiler_params=pltpu.CompilerParams(
            collective_id=0, has_side_effects=True, vmem_limit_bytes=56 * 1024 * 1024
        ),
        cost_estimate=pl.CostEstimate(flops=4_000_000_000, bytes_accessed=10_000_000, transcendentals=0),
    )(taps.reshape(4, 2048, 512), ln_gain, w_proj, conv_one, conv_two.T)
    return out.reshape(4, 8, 32, 64).transpose(0, 1, 3, 2)


def solution(mesh):
    placed = (
        P(None, "dp", "mp", None, "section"),
        P(None, "section"),
        P(None, ("section", "dp", "mp"), None),
        P(("dp", "mp"), None),
        P(("dp", "mp"), "section"),
    )
    return jax.shard_map(
        per_device,
        mesh=mesh,
        in_specs=placed,
        out_specs=P("dp", "mp", None, "section"),
        check_vma=False,
    )
```

```python
import jax
import jax.numpy as jnp
from jax import lax
from jax.experimental import pallas as pl
from jax.experimental.pallas import tpu as pltpu
from jax.sharding import PartitionSpec as P

D = 4096
TAPS = 4
MESH = pl.DeviceIdType.MESH
F32 = jnp.float32
BF16 = jnp.bfloat16
N_COPIES = 112


class Links:
    def __init__(self, send_sems, recv_sems):
        self.send_sems, self.recv_sems = send_sems, recv_sems
        self.used = 0
        self.copies = []

    def make(self, src, dst, to, recv_sem=None):
        copy = pltpu.make_async_remote_copy(
            src_ref=src,
            dst_ref=dst,
            send_sem=self.send_sems.at[self.used],
            recv_sem=self.recv_sems.at[self.used] if recv_sem is None else recv_sem,
            device_id=to,
            device_id_type=MESH,
        )
        self.used += 1
        return copy

    def start(self, src, dst, to, recv_sem=None):
        copy = self.make(src, dst, to, recv_sem)
        copy.start()
        self.copies.append(copy)
        return copy

    def sent(self, copy):
        copy.wait_send()
        self.copies = [c for c in self.copies if c is not copy]

    def finish(self):
        for copy in self.copies:
            copy.wait_send()


def received(copies):
    for copy in copies:
        copy.wait_recv()


def kernel(
    taps_hbm, gain_ref, w_ref, c1_ref, c2_ref, out_ref,
    taps, part, wall, gw, gsum, gcol, gains, c2sq, c2pad, c2all, call_, conv, tot, tparts, tall, tcols,
    joint, jsib, jsum, jrecv, act, hsib, hcross, x1, x2, res, packed, arrived,
    tap_sems, send_sems, recv_sems,
):
    sec, x, mp = lax.axis_index("section"), lax.axis_index("dp"), lax.axis_index("mp")
    zlo, core = sec // 2, sec % 2
    zhi, y = mp // 4, mp % 4
    links = Links(send_sems, recv_sems)

    reads = [pltpu.make_async_copy(taps_hbm.at[t], taps.at[t], tap_sems.at[t]) for t in range(TAPS)]
    for read in reads:
        read.start()

    peers = [{"section": (sec + k) % 8} for k in range(1, 8)]
    xs = [{"dp": (x + k) % 4} for k in (1, 3, 2)]
    ys = [{"mp": zhi * 4 + (y + k) % 4} for k in (1, 3, 2)]
    z_far = {"mp": (1 - zhi) * 4 + y}
    sibling = {"section": zlo * 2 + 1 - core}
    has_cross = jnp.where(core == 0, mp > 0, mp < 7)
    cross = {"mp": (mp + 7 + 2 * core) % 8, "section": zlo * 2 + 1 - core}

    hcross[...] = jnp.zeros_like(hcross)

    barrier = pltpu.get_barrier_semaphore()
    greeted = peers + xs + ys + [z_far]
    for device in greeted:
        pl.semaphore_signal(barrier, inc=1, device_id=device, device_id_type=MESH)

    @pl.when(has_cross)
    def _():
        pl.semaphore_signal(barrier, inc=1, device_id=cross, device_id_type=MESH)

    for t in range(TAPS):
        wall[t, x, zhi, y] = w_ref[t]
    pl.semaphore_wait(barrier, len(greeted) + has_cross.astype(jnp.int32))

    every = slice(None)

    def w_view(half, xi, yi, zi):
        return wall.at[2 * half : 2 * half + 2, xi, zi, yi]

    def c_view(half, xi, yi, zi):
        return call_.at[core, xi, zi, yi, (slice(0, 48), slice(48, 80))[half]]

    def first(view, zi):
        got = []
        for half, to in ((0, xs), (1, ys)):
            s = view(half, x, y, zi)
            got.append([links.start(s, s, device) for device in to])
        return got

    def second(view, zi, got):
        sent = []
        received(got[0])
        s = view(0, every, y, zi)
        sent += [links.start(s, s, device) for device in ys]
        received(got[1])
        s = view(1, x, every, zi)
        sent += [links.start(s, s, device) for device in xs]
        return sent

    mine = wall.at[:, x, zhi, y]
    w_far = links.start(mine, mine, z_far)
    w_near = first(w_view, zhi)

    lane = lax.broadcasted_iota(jnp.int32, (128, 128), 1)

    def stats(t, total):
        reads[t].wait()
        v = taps[t].astype(F32)
        s = jnp.sum(v, axis=1, keepdims=True)
        q = jnp.sum(v * v, axis=1, keepdims=True)
        for b in range(16):
            total = jnp.where(lane == b * 8 + t, s[128 * b : 128 * b + 128], total)
            total = jnp.where(lane == b * 8 + 4 + t, q[128 * b : 128 * b + 128], total)
        return total

    c2sq[...] = jnp.zeros_like(c2sq)
    c2sq[0:32, 0:72] = c2_ref[...].astype(F32)
    rows = c2sq[...].T
    c2pad[...] = jnp.concatenate(
        [rows[0:24] + pltpu.roll(rows[24:48], 32, 1) + pltpu.roll(rows[48:72], 64, 1), jnp.zeros((8, 128), F32)], axis=0
    ).astype(BF16)
    gcol[...] = jnp.zeros_like(gcol)
    gcol[0:4, :] = gain_ref[...]
    c2_got = [links.start(c2pad, c2all.at[k], peers[k - 1]) for k in range(1, 8)]

    gains[...] = gcol[...].T
    total = jnp.zeros((128, 128), F32)
    for t in range(3):
        total = stats(t, total)
    w_far.wait_recv()
    w_far = first(w_view, 1 - zhi)
    w_near = second(w_view, zhi, w_near)
    total = stats(3, total)
    tot[...] = total.T.reshape(8, 16, 128)
    sent = [links.start(tot.at[(sec + k) % 8], tparts.at[k], peers[k - 1]) for k in range(1, 8)]

    received(c2_got)
    c2all[0] = c2pad[...]
    lanes24 = lax.broadcasted_iota(jnp.int32, (24, 128), 1) // 32
    sides = [[jnp.zeros((24, 128), F32) for _ in range(3)] for _ in range(2)]
    for d in range(8):
        block = c2all[(sec - d + 8) % 8].astype(F32)[0:24]
        for g in range(3):
            turn = (32 * (d % 4 - g)) % 128
            moved = pltpu.roll(block, turn, 1) if turn else block
            sides[d // 4][g] = jnp.where(lanes24 == d % 4, moved, sides[d // 4][g])
    blank = jnp.zeros((8, 256), F32)
    one = jnp.concatenate([c1_ref[...].astype(F32), blank], axis=0)
    two = jnp.concatenate([jnp.concatenate(side, axis=0) for side in sides], axis=1)
    two = jnp.concatenate([two, blank], axis=0)
    call_[core, x, zhi, y] = jnp.where(core == 0, one, two).astype(BF16)
    mine = call_.at[core, x, zhi, y]
    c_far = links.start(mine, mine, z_far)
    w_far = second(w_view, 1 - zhi, w_far)

    received(sent)
    own = tot[sec]
    for k in range(1, 8):
        own = own + tparts[k]
    outs = []
    for blk in range(2):
        mean = own[8 * blk : 8 * blk + 4] / D
        var = jnp.maximum(own[8 * blk + 4 : 8 * blk + 8] / D - mean * mean, 0.0)
        r = lax.rsqrt(var + 1e-6)
        outs += [r, r * mean]
    tall[sec] = jnp.concatenate(outs, axis=0)
    mine = tall.at[sec]
    sent = [links.start(mine, mine, peers[k - 1]) for k in range(1, 8)]

    def scale(zi):
        for t in range(TAPS):
            sums = jnp.zeros((1, 256), F32)
            for i in range(4):
                rows = pl.ds(pl.multiple_of(i * 128 + zi * 64, 64), 64)
                piece = wall[t, i, zi].reshape(64, 256).astype(F32) * gains[rows, t : t + 1]
                piece = piece.astype(BF16)
                gw[t, rows, :] = piece
                sums = sums + jnp.sum(piece.astype(F32), axis=0, keepdims=True)
            gsum[t] = gsum[t] + sums

    gsum[...] = jnp.zeros_like(gsum)
    received(w_near)
    scale(zhi)
    c_far.wait_recv()
    c_got = first(c_view, every)
    received(w_far)
    scale(1 - zhi)
    received(sent)
    tcols[...] = tall[...].reshape(128, 128).T

    def strip(image, half):
        rows = pl.ds(pl.multiple_of(image * 512 + half * 256, 256), 256)
        for t in range(TAPS):
            part[t] = jnp.dot(taps[t, rows, :], gw[t], preferred_element_type=F32)
        for blk in range(2):
            cols = pltpu.roll(tcols[...], (128 - 8 * (image * 4 + half * 2 + blk)) % 128, 1)
            span = slice(blk * 128, blk * 128 + 128)
            acc = cols[:, 0:1] * part[0, span, :] - cols[:, 4:5] * gsum[0]
            for t in range(1, TAPS):
                acc = acc + (cols[:, t : t + 1] * part[t, span, :] - cols[:, 4 + t : 5 + t] * gsum[t])
            joint[image, half, span] = acc.astype(BF16)

    images = [(zlo + k) % 4 for k in range(4)]
    z_sent = {}
    swaps = {}

    def swap(k):
        strip(images[k], 1 - core)
        swaps[k] = links.start(joint.at[images[k], 1 - core], jsib.at[k], sibling)

    def pair(k, h):
        span = pl.ds(pl.multiple_of(128 * h, 128), 128)
        return joint[images[k], core, span].astype(F32) + jsib[k, span].astype(F32)

    def onward(k, i):
        h = halves[i]
        jsum[k, h] = pair(k, h).astype(BF16)
        z_sent[k, i] = links.start(jsum.at[k, h], jrecv.at[k, h], {"section": (sec + 2 * k) % 8})

    def joined(i):
        h = halves[i]
        value = pair(0, h)
        for k in range(1, 4):
            z_sent[k, i].wait_recv()
            value = value + jrecv[k, h].astype(F32)
        res[h] = value
        act[h] = jnp.maximum(value, 0.0).astype(BF16)

    def unpack(which):
        def body(i, _):
            for j in range(2):
                for l in (0, 2):
                    one = call_[which, i, j, l].astype(F32)[0:72]
                    two = call_[which, i, j, l + 1].astype(F32)[0:72]
                    at = pl.ds(pl.multiple_of(i * 576, 16) + 288 * j + 72 * l, 144)
                    conv[which, at, :] = jnp.concatenate([one, two], axis=0).astype(BF16)
            return 0

        lax.fori_loop(0, 4, body, 0)

    halves = (core, 1 - core)
    swap(1)
    swap(2)
    strip(images[1], core)
    swap(3)
    swaps[1].wait_recv()
    onward(1, 0)
    c_got = second(c_view, every, c_got)
    strip(images[2], core)
    swaps[2].wait_recv()
    onward(2, 0)
    strip(images[3], core)
    swaps[3].wait_recv()
    onward(3, 0)
    swap(0)
    for k in (1, 2, 3):
        links.sent(z_sent[k, 0])
        onward(k, 1)
    strip(images[0], core)
    swaps[0].wait_recv()
    joined(0)
    h2 = links.make(act.at[core], hcross, cross)

    @pl.when(has_cross)
    def _():
        h2.start()

    received(c_got)
    whole = call_.at[core]
    c_swap = links.start(whole, whole, sibling)
    unpack(core)
    joined(1)
    h1 = links.start(act.at[1 - core], hsib, sibling)
    c_swap.wait_recv()
    unpack(1 - core)

    def columns(value, x_ref, start):
        rows = value.shape[0]
        span = pl.ds(pl.multiple_of(start, 64), rows)
        col = lax.broadcasted_iota(jnp.int32, (rows, 256), 0) % 64
        x_ref[span, 0:256] = jnp.where(col == 0, 0.0, pltpu.roll(value, 1, 0)).astype(BF16)
        x_ref[span, 256:512] = value.astype(BF16)
        x_ref[span, 512:768] = jnp.where(col == 63, 0.0, pltpu.roll(value, rows - 1, 0)).astype(BF16)

    def convolved(x_ref, which, start, rows):
        total = jnp.zeros((rows, 256), F32)
        for a in range(3):
            span = pl.ds(pl.multiple_of(start + 64 * a, 64), rows)
            total = total + jnp.dot(
                x_ref[span], conv[which, 768 * a : 768 * a + 768], preferred_element_type=F32
            )
        return total

    def finished(which_half, p):
        total = convolved(x2, 1, 128 * which_half, 128) + res[which_half]
        packed[p] = total.T.astype(BF16).reshape(8, 32, 128)
        return [links.start(packed.at[p, (sec + k) % 8], arrived.at[p, k], peers[k - 1]) for k in range(1, 8)]

    columns(jnp.maximum(res[...].reshape(256, 256), 0.0), x1, 128)
    h1.wait_recv()
    columns(hsib[...].astype(F32), x1, 384 * (1 - core))
    columns(jnp.maximum(convolved(x1, 0, 128 * (1 - core), 256), 0.0), x2, 128 * (1 - core))
    outs = [finished(1 - core, 0)]

    @pl.when(has_cross)
    def _():
        h2.wait_recv()
        h2.wait_send()

    columns(hcross[...].astype(F32), x1, 384 * core)
    row = lax.broadcasted_iota(jnp.int32, (128, 256), 0) // 64
    outside = jnp.logical_and(row == core, jnp.logical_not(has_cross))
    mid = jnp.where(outside, 0.0, jnp.maximum(convolved(x1, 0, 256 * core, 128), 0.0))
    columns(mid, x2, 256 * core)
    outs.append(finished(core, 1))

    for p in range(2):
        arrived[p, 0] = packed[p, sec]
        for k in range(8):
            if k:
                outs[p][k - 1].wait_recv()
            their = (core + k) % 2
            block = arrived[p, k].astype(F32)
            for r, rows in ((0, block), (1, pltpu.roll(block, 64, 1))):
                at = 64 * (1 - their if p == 0 else their) + 32 * r
                out_ref[(sec - k + 8) % 8, pl.ds(pl.multiple_of(at, 32), 32), :] = rows[:, 0:64].astype(BF16)
    links.finish()


def per_device(taps, ln_gain, w_proj, conv_one, conv_two):
    vmem = pl.BlockSpec(memory_space=pltpu.VMEM)
    out = pl.pallas_call(
        kernel,
        out_shape=jax.ShapeDtypeStruct((8, 128, 64), BF16),
        in_specs=[pl.BlockSpec(memory_space=pl.ANY)] + [vmem] * 4,
        out_specs=vmem,
        scratch_shapes=[
            pltpu.VMEM((4, 2048, 512), BF16),
            pltpu.VMEM((4, 256, 256), F32),
            pltpu.VMEM((4, 4, 2, 4, 16, 256), BF16),
            pltpu.VMEM((4, 512, 256), BF16),
            pltpu.VMEM((4, 1, 256), F32),
            pltpu.VMEM((128, 512), F32),
            pltpu.VMEM((512, 128), F32),
            pltpu.VMEM((128, 128), F32),
            pltpu.VMEM((32, 128), BF16),
            pltpu.VMEM((8, 32, 128), BF16),
            pltpu.VMEM((2, 4, 2, 4, 80, 256), BF16),
            pltpu.VMEM((2, 2304, 256), BF16),
            pltpu.VMEM((8, 16, 128), F32),
            pltpu.VMEM((8, 16, 128), F32),
            pltpu.VMEM((8, 16, 128), F32),
            pltpu.VMEM((128, 128), F32),
            pltpu.VMEM((4, 2, 256, 256), BF16),
            pltpu.VMEM((4, 256, 256), BF16),
            pltpu.VMEM((4, 2, 128, 256), BF16),
            pltpu.VMEM((4, 2, 128, 256), BF16),
            pltpu.VMEM((2, 128, 256), BF16),
            pltpu.VMEM((128, 256), BF16),
            pltpu.VMEM((128, 256), BF16),
            pltpu.VMEM((512, 768), BF16),
            pltpu.VMEM((384, 768), BF16),
            pltpu.VMEM((2, 128, 256), F32),
            pltpu.VMEM((2, 8, 32, 128), BF16),
            pltpu.VMEM((2, 8, 32, 128), BF16),
            pltpu.SemaphoreType.DMA((TAPS,)),
            pltpu.SemaphoreType.DMA((N_COPIES,)),
            pltpu.SemaphoreType.DMA((N_COPIES,)),
        ],
        compiler_params=pltpu.CompilerParams(
            collective_id=0, has_side_effects=True, vmem_limit_bytes=56 * 1024 * 1024
        ),
        cost_estimate=pl.CostEstimate(flops=4_000_000_000, bytes_accessed=10_000_000, transcendentals=0),
    )(taps.reshape(4, 2048, 512), ln_gain, w_proj, conv_one, conv_two.T)
    return out.reshape(4, 8, 32, 64).transpose(0, 1, 3, 2)


def solution(mesh):
    placed = (
        P(None, "dp", "mp", None, "section"),
        P(None, "section"),
        P(None, ("section", "dp", "mp"), None),
        P(("dp", "mp"), None),
        P(("dp", "mp"), "section"),
    )
    return jax.shard_map(
        per_device,
        mesh=mesh,
        in_specs=placed,
        out_specs=P("dp", "mp", None, "section"),
        check_vma=False,
    )
```

```python
import jax
import jax.numpy as jnp
from jax import lax
from jax.experimental import pallas as pl
from jax.experimental.pallas import tpu as pltpu
from jax.sharding import PartitionSpec as P

D = 4096
TAPS = 4
MESH = pl.DeviceIdType.MESH
F32 = jnp.float32
BF16 = jnp.bfloat16
N_COPIES = 112


class Links:
    def __init__(self, send_sems, recv_sems):
        self.send_sems, self.recv_sems = send_sems, recv_sems
        self.used = 0
        self.copies = []

    def make(self, src, dst, to, recv_sem=None):
        copy = pltpu.make_async_remote_copy(
            src_ref=src,
            dst_ref=dst,
            send_sem=self.send_sems.at[self.used],
            recv_sem=self.recv_sems.at[self.used] if recv_sem is None else recv_sem,
            device_id=to,
            device_id_type=MESH,
        )
        self.used += 1
        return copy

    def start(self, src, dst, to, recv_sem=None):
        copy = self.make(src, dst, to, recv_sem)
        copy.start()
        self.copies.append(copy)
        return copy

    def sent(self, copy):
        copy.wait_send()
        self.copies = [c for c in self.copies if c is not copy]

    def finish(self):
        for copy in self.copies:
            copy.wait_send()


def received(copies):
    for copy in copies:
        copy.wait_recv()


def kernel(
    taps_hbm, gain_ref, w_ref, c1_ref, c2_ref, out_ref,
    taps, part, wall, gw, gsum, gcol, gains, c2sq, c2pad, c2all, call_, conv, tot, tparts, tall, tcols,
    joint, jsib, jsum, jrecv, act, hsib, hcross, x1, x2, res, packed, arrived,
    tap_sems, send_sems, recv_sems,
):
    sec, x, mp = lax.axis_index("section"), lax.axis_index("dp"), lax.axis_index("mp")
    zlo, core = sec // 2, sec % 2
    zhi, y = mp // 4, mp % 4
    links = Links(send_sems, recv_sems)

    reads = [pltpu.make_async_copy(taps_hbm.at[t], taps.at[t], tap_sems.at[t]) for t in range(TAPS)]
    for read in reads:
        read.start()

    peers = [{"section": (sec + k) % 8} for k in range(1, 8)]
    xs = [{"dp": (x + k) % 4} for k in (1, 3, 2)]
    ys = [{"mp": zhi * 4 + (y + k) % 4} for k in (1, 3, 2)]
    z_far = {"mp": (1 - zhi) * 4 + y}
    sibling = {"section": zlo * 2 + 1 - core}
    has_cross = jnp.where(core == 0, mp > 0, mp < 7)
    cross = {"mp": (mp + 7 + 2 * core) % 8, "section": zlo * 2 + 1 - core}

    hcross[...] = jnp.zeros_like(hcross)

    barrier = pltpu.get_barrier_semaphore()
    greeted = peers + xs + ys + [z_far]
    for device in greeted:
        pl.semaphore_signal(barrier, inc=1, device_id=device, device_id_type=MESH)

    @pl.when(has_cross)
    def _():
        pl.semaphore_signal(barrier, inc=1, device_id=cross, device_id_type=MESH)

    for t in range(TAPS):
        wall[t, x, zhi, y] = w_ref[t]
    pl.semaphore_wait(barrier, len(greeted) + has_cross.astype(jnp.int32))

    every = slice(None)

    def everyone(refs):
        copies = {k: links.start(*refs(k), peers[k - 1]) for k in (4, 3, 5, 2, 6, 1, 7)}
        return [copies[k] for k in range(1, 8)]


    def w_view(half, xi, yi, zi):
        return wall.at[2 * half : 2 * half + 2, xi, zi, yi]

    def c_view(half, xi, yi, zi):
        return call_.at[core, xi, zi, yi, (slice(0, 48), slice(48, 80))[half]]

    def first(view, zi):
        got = []
        for half, to in ((0, xs), (1, ys)):
            s = view(half, x, y, zi)
            got.append([links.start(s, s, device) for device in to])
        return got

    def second(view, zi, got):
        sent = []
        received(got[0])
        s = view(0, every, y, zi)
        sent += [links.start(s, s, device) for device in ys]
        received(got[1])
        s = view(1, x, every, zi)
        sent += [links.start(s, s, device) for device in xs]
        return sent

    mine = wall.at[:, x, zhi, y]
    w_far = links.start(mine, mine, z_far)
    w_near = first(w_view, zhi)

    lane = lax.broadcasted_iota(jnp.int32, (128, 128), 1)

    def stats(t, total):
        reads[t].wait()
        v = taps[t].astype(F32)
        s = jnp.sum(v, axis=1, keepdims=True)
        q = jnp.sum(v * v, axis=1, keepdims=True)
        for b in range(16):
            total = jnp.where(lane == b * 8 + t, s[128 * b : 128 * b + 128], total)
            total = jnp.where(lane == b * 8 + 4 + t, q[128 * b : 128 * b + 128], total)
        return total

    c2sq[...] = jnp.zeros_like(c2sq)
    c2sq[0:32, 0:72] = c2_ref[...].astype(F32)
    rows = c2sq[...].T
    c2pad[...] = jnp.concatenate(
        [rows[0:24] + pltpu.roll(rows[24:48], 32, 1) + pltpu.roll(rows[48:72], 64, 1), jnp.zeros((8, 128), F32)], axis=0
    ).astype(BF16)
    gcol[...] = jnp.zeros_like(gcol)
    gcol[0:4, :] = gain_ref[...]
    c2_got = [links.start(c2pad, c2all.at[k], peers[k - 1]) for k in range(1, 8)]

    gains[...] = gcol[...].T
    total = jnp.zeros((128, 128), F32)
    for t in range(3):
        total = stats(t, total)
    w_far.wait_recv()
    w_far = first(w_view, 1 - zhi)
    w_near = second(w_view, zhi, w_near)
    total = stats(3, total)
    tot[...] = total.T.reshape(8, 16, 128)
    sent = everyone(lambda k: (tot.at[(sec + k) % 8], tparts.at[k]))

    received(c2_got)
    c2all[0] = c2pad[...]
    lanes24 = lax.broadcasted_iota(jnp.int32, (24, 128), 1) // 32
    sides = [[jnp.zeros((24, 128), F32) for _ in range(3)] for _ in range(2)]
    for d in range(8):
        block = c2all[(sec - d + 8) % 8].astype(F32)[0:24]
        for g in range(3):
            turn = (32 * (d % 4 - g)) % 128
            moved = pltpu.roll(block, turn, 1) if turn else block
            sides[d // 4][g] = jnp.where(lanes24 == d % 4, moved, sides[d // 4][g])
    blank = jnp.zeros((8, 256), F32)
    one = jnp.concatenate([c1_ref[...].astype(F32), blank], axis=0)
    two = jnp.concatenate([jnp.concatenate(side, axis=0) for side in sides], axis=1)
    two = jnp.concatenate([two, blank], axis=0)
    call_[core, x, zhi, y] = jnp.where(core == 0, one, two).astype(BF16)
    mine = call_.at[core, x, zhi, y]
    c_far = links.start(mine, mine, z_far)
    w_far = second(w_view, 1 - zhi, w_far)

    received(sent)
    own = tot[sec]
    for k in range(1, 8):
        own = own + tparts[k]
    outs = []
    for blk in range(2):
        mean = own[8 * blk : 8 * blk + 4] / D
        var = jnp.maximum(own[8 * blk + 4 : 8 * blk + 8] / D - mean * mean, 0.0)
        r = lax.rsqrt(var + 1e-6)
        outs += [r, r * mean]
    tall[sec] = jnp.concatenate(outs, axis=0)
    mine = tall.at[sec]
    sent = everyone(lambda k: (mine, mine))

    def scale(zi):
        for t in range(TAPS):
            sums = jnp.zeros((1, 256), F32)
            for i in range(4):
                rows = pl.ds(pl.multiple_of(i * 128 + zi * 64, 64), 64)
                piece = wall[t, i, zi].reshape(64, 256).astype(F32) * gains[rows, t : t + 1]
                piece = piece.astype(BF16)
                gw[t, rows, :] = piece
                sums = sums + jnp.sum(piece.astype(F32), axis=0, keepdims=True)
            gsum[t] = gsum[t] + sums

    gsum[...] = jnp.zeros_like(gsum)
    received(w_near)
    scale(zhi)
    c_far.wait_recv()
    c_got = first(c_view, every)
    received(w_far)
    scale(1 - zhi)
    received(sent)
    tcols[...] = tall[...].reshape(128, 128).T

    def strip(image, half):
        rows = pl.ds(pl.multiple_of(image * 512 + half * 256, 256), 256)
        for t in range(TAPS):
            part[t] = jnp.dot(taps[t, rows, :], gw[t], preferred_element_type=F32)
        for blk in range(2):
            cols = pltpu.roll(tcols[...], (128 - 8 * (image * 4 + half * 2 + blk)) % 128, 1)
            span = slice(blk * 128, blk * 128 + 128)
            acc = cols[:, 0:1] * part[0, span, :] - cols[:, 4:5] * gsum[0]
            for t in range(1, TAPS):
                acc = acc + (cols[:, t : t + 1] * part[t, span, :] - cols[:, 4 + t : 5 + t] * gsum[t])
            joint[image, half, span] = acc.astype(BF16)

    images = [(zlo + k) % 4 for k in range(4)]
    z_sent = {}
    swaps = {}

    def swap(k):
        strip(images[k], 1 - core)
        swaps[k] = links.start(joint.at[images[k], 1 - core], jsib.at[k], sibling)

    def pair(k, h):
        span = pl.ds(pl.multiple_of(128 * h, 128), 128)
        return joint[images[k], core, span].astype(F32) + jsib[k, span].astype(F32)

    def onward(k, i):
        h = halves[i]
        jsum[k, h] = pair(k, h).astype(BF16)
        z_sent[k, i] = links.start(jsum.at[k, h], jrecv.at[k, h], {"section": (sec + 2 * k) % 8})

    def joined(i):
        h = halves[i]
        value = pair(0, h)
        for k in range(1, 4):
            z_sent[k, i].wait_recv()
            value = value + jrecv[k, h].astype(F32)
        res[h] = value
        act[h] = jnp.maximum(value, 0.0).astype(BF16)

    def unpack(which):
        def body(i, _):
            for j in range(2):
                for l in (0, 2):
                    one = call_[which, i, j, l].astype(F32)[0:72]
                    two = call_[which, i, j, l + 1].astype(F32)[0:72]
                    at = pl.ds(pl.multiple_of(i * 576, 16) + 288 * j + 72 * l, 144)
                    conv[which, at, :] = jnp.concatenate([one, two], axis=0).astype(BF16)
            return 0

        lax.fori_loop(0, 4, body, 0)

    halves = (core, 1 - core)
    swap(1)
    swap(2)
    strip(images[1], core)
    swap(3)
    swaps[1].wait_recv()
    onward(1, 0)
    c_got = second(c_view, every, c_got)
    strip(images[2], core)
    swaps[2].wait_recv()
    onward(2, 0)
    strip(images[3], core)
    swaps[3].wait_recv()
    onward(3, 0)
    swap(0)
    for k in (1, 2, 3):
        links.sent(z_sent[k, 0])
        onward(k, 1)
    strip(images[0], core)
    swaps[0].wait_recv()
    joined(0)
    h2 = links.make(act.at[core], hcross, cross)

    @pl.when(has_cross)
    def _():
        h2.start()

    received(c_got)
    whole = call_.at[core]
    c_swap = links.start(whole, whole, sibling)
    unpack(core)
    joined(1)
    h1 = links.start(act.at[1 - core], hsib, sibling)
    c_swap.wait_recv()
    unpack(1 - core)

    def columns(value, x_ref, start):
        rows = value.shape[0]
        span = pl.ds(pl.multiple_of(start, 64), rows)
        col = lax.broadcasted_iota(jnp.int32, (rows, 256), 0) % 64
        x_ref[span, 0:256] = jnp.where(col == 0, 0.0, pltpu.roll(value, 1, 0)).astype(BF16)
        x_ref[span, 256:512] = value.astype(BF16)
        x_ref[span, 512:768] = jnp.where(col == 63, 0.0, pltpu.roll(value, rows - 1, 0)).astype(BF16)

    def convolved(x_ref, which, start, rows):
        total = jnp.zeros((rows, 256), F32)
        for a in range(3):
            span = pl.ds(pl.multiple_of(start + 64 * a, 64), rows)
            total = total + jnp.dot(
                x_ref[span], conv[which, 768 * a : 768 * a + 768], preferred_element_type=F32
            )
        return total

    def finished(which_half, p):
        total = convolved(x2, 1, 128 * which_half, 128) + res[which_half]
        packed[p] = total.T.astype(BF16).reshape(8, 32, 128)
        return everyone(lambda k: (packed.at[p, (sec + k) % 8], arrived.at[p, k]))

    columns(jnp.maximum(res[...].reshape(256, 256), 0.0), x1, 128)
    h1.wait_recv()
    columns(hsib[...].astype(F32), x1, 384 * (1 - core))
    columns(jnp.maximum(convolved(x1, 0, 128 * (1 - core), 256), 0.0), x2, 128 * (1 - core))
    outs = [finished(1 - core, 0)]

    @pl.when(has_cross)
    def _():
        h2.wait_recv()
        h2.wait_send()

    columns(hcross[...].astype(F32), x1, 384 * core)
    row = lax.broadcasted_iota(jnp.int32, (128, 256), 0) // 64
    outside = jnp.logical_and(row == core, jnp.logical_not(has_cross))
    mid = jnp.where(outside, 0.0, jnp.maximum(convolved(x1, 0, 256 * core, 128), 0.0))
    columns(mid, x2, 256 * core)
    outs.append(finished(core, 1))

    for p in range(2):
        arrived[p, 0] = packed[p, sec]
        for k in (0, 1, 7, 2, 6, 3, 5, 4):
            if k:
                outs[p][k - 1].wait_recv()
            their = (core + k) % 2
            block = arrived[p, k].astype(F32)
            for r, rows in ((0, block), (1, pltpu.roll(block, 64, 1))):
                at = 64 * (1 - their if p == 0 else their) + 32 * r
                out_ref[(sec - k + 8) % 8, pl.ds(pl.multiple_of(at, 32), 32), :] = rows[:, 0:64].astype(BF16)
    links.finish()


def per_device(taps, ln_gain, w_proj, conv_one, conv_two):
    vmem = pl.BlockSpec(memory_space=pltpu.VMEM)
    out = pl.pallas_call(
        kernel,
        out_shape=jax.ShapeDtypeStruct((8, 128, 64), BF16),
        in_specs=[pl.BlockSpec(memory_space=pl.ANY)] + [vmem] * 4,
        out_specs=vmem,
        scratch_shapes=[
            pltpu.VMEM((4, 2048, 512), BF16),
            pltpu.VMEM((4, 256, 256), F32),
            pltpu.VMEM((4, 4, 2, 4, 16, 256), BF16),
            pltpu.VMEM((4, 512, 256), BF16),
            pltpu.VMEM((4, 1, 256), F32),
            pltpu.VMEM((128, 512), F32),
            pltpu.VMEM((512, 128), F32),
            pltpu.VMEM((128, 128), F32),
            pltpu.VMEM((32, 128), BF16),
            pltpu.VMEM((8, 32, 128), BF16),
            pltpu.VMEM((2, 4, 2, 4, 80, 256), BF16),
            pltpu.VMEM((2, 2304, 256), BF16),
            pltpu.VMEM((8, 16, 128), F32),
            pltpu.VMEM((8, 16, 128), F32),
            pltpu.VMEM((8, 16, 128), F32),
            pltpu.VMEM((128, 128), F32),
            pltpu.VMEM((4, 2, 256, 256), BF16),
            pltpu.VMEM((4, 256, 256), BF16),
            pltpu.VMEM((4, 2, 128, 256), BF16),
            pltpu.VMEM((4, 2, 128, 256), BF16),
            pltpu.VMEM((2, 128, 256), BF16),
            pltpu.VMEM((128, 256), BF16),
            pltpu.VMEM((128, 256), BF16),
            pltpu.VMEM((512, 768), BF16),
            pltpu.VMEM((384, 768), BF16),
            pltpu.VMEM((2, 128, 256), F32),
            pltpu.VMEM((2, 8, 32, 128), BF16),
            pltpu.VMEM((2, 8, 32, 128), BF16),
            pltpu.SemaphoreType.DMA((TAPS,)),
            pltpu.SemaphoreType.DMA((N_COPIES,)),
            pltpu.SemaphoreType.DMA((N_COPIES,)),
        ],
        compiler_params=pltpu.CompilerParams(
            collective_id=0, has_side_effects=True, vmem_limit_bytes=56 * 1024 * 1024
        ),
        cost_estimate=pl.CostEstimate(flops=4_000_000_000, bytes_accessed=10_000_000, transcendentals=0),
    )(taps.reshape(4, 2048, 512), ln_gain, w_proj, conv_one, conv_two.T)
    return out.reshape(4, 8, 32, 64).transpose(0, 1, 3, 2)


def solution(mesh):
    placed = (
        P(None, "dp", "mp", None, "section"),
        P(None, "section"),
        P(None, ("section", "dp", "mp"), None),
        P(("dp", "mp"), None),
        P(("dp", "mp"), "section"),
    )
    return jax.shard_map(
        per_device,
        mesh=mesh,
        in_specs=placed,
        out_specs=P("dp", "mp", None, "section"),
        check_vma=False,
    )
```
